32 devices in a mesh: section: 4 (over z), tensor: 8 (over y, x, core).
Axes of the slice: x: 2, y: 2, z: 4, core: 2. Of those that a mesh axis runs over, the one named last changes fastest.
Arguments:
- tokens: bfloat16 [192, 6144], P('tensor', 'section'), may hold values from -6 to 6
- combine: float32 [192, 2], replicated, may hold values from 0.1 to 1
- expert_ids: int32 [192, 2], replicated, may hold values from 0 to 3, as said below
- expert_counts: int32 [4], replicated, may hold values from 0 to 192, as said below
- w_gate: bfloat16 [4, 6144, 16384], P(None, 'section', 'tensor'), may hold values from -0.078125 to 0.078125
- w_up: bfloat16 [4, 6144, 16384], P(None, 'section', 'tensor'), may hold values from -0.078125 to 0.078125
- w_down: bfloat16 [4, 16384, 6144], P(None, 'tensor', 'section'), may hold values from -0.046875 to 0.046875
- cotangent: bfloat16 [192, 6144], P('tensor', 'section'), may hold values from -6 to 6
Outputs:
- layer_out: bfloat16 [192, 6144], P('tensor', 'section')
- d_tokens: bfloat16 [192, 6144], P('tensor', 'section')
- d_down: bfloat16 [4, 16384, 6144], P(None, 'tensor', 'section')
The draws below stay inside these ranges and needn't reach their ends.
Inputs may be any that keep to these rules, and one draw needn't show every extreme that they name: `expert_ids`: each row names two different experts; one expert, drawn from the seed, is named by every row. expert_counts[e] is the number of entries of expert_ids equal to e.
All inputs are finite; a program needn't handle non-finite values.
Results may differ from the reference program's by a relative error of at most 0.0058.
Values may be sent and summed in bfloat16 or wider, within the bound.
No kernel may reach another device: no remote copies, remote signals or barrier semaphores. Data moves between devices by JAX's collectives and lax.ppermute only.
A program may use at most 320 MiB of HBM per device.

```python
import jax
import jax.numpy as jnp
from jax import lax

D = 6144
FF = 16384
EXPERTS = 4
BLOCK = 128
TOKENS = 192


def assignments(key):
    base = jax.random.fold_in(key, 17)
    first_key, second_key, label_key = jax.random.split(base, 3)
    first_raw = jax.random.randint(first_key, (TOKENS,), 0, 2 * EXPERTS)
    first_code = jnp.where(first_raw >= EXPERTS, 0, first_raw)
    labels = jax.random.permutation(label_key, EXPERTS)
    first = labels[first_code]
    other = labels[(first_code * 0 + jax.random.randint(second_key, (TOKENS,), 1, EXPERTS)) % EXPERTS]
    second = jnp.where(first_code == 0, other, labels[0])
    return jnp.stack([first, second], 1).astype(jnp.int32)


def draw_expert_ids(key, part):
    return assignments(key)


def draw_expert_counts(key, part):
    chosen = assignments(key).reshape(-1)
    onehot = (chosen[:, None] == jnp.arange(EXPERTS)[None, :]).astype(jnp.int32)
    return jnp.sum(onehot, 0).astype(jnp.int32)


def shard_levels(rng, extent, cuts, least, largest):
    level = 1.0
    for axis_at, blocks in cuts:
        steps = jax.random.uniform(jax.random.fold_in(jax.random.fold_in(rng, 6), axis_at), (blocks,), jnp.float32, least / len(cuts), largest / len(cuts))
        level = level * jnp.repeat(jnp.exp(steps), extent[axis_at] // blocks).reshape((-1,) + (1,) * (len(extent) - 1 - axis_at))
    return level


def noise(rng, extent, width, limit, cuts=(), kind=jnp.bfloat16):
    gain = shard_levels(rng, extent, cuts, -0.22, 0.18) if cuts else 1.0
    values = jax.random.normal(rng, extent, jnp.float32) * width * gain
    return jnp.minimum(jnp.maximum(values, -limit), limit).astype(kind)


def setup_inputs(seed: int = 0) -> dict:
    keys = jax.random.split(jax.random.key(seed), 9)
    tokens = noise(keys[0], (TOKENS, D), 1.0, 6.0, ((0, 8), (1, 4)))
    combine = jnp.clip(jax.random.uniform(keys[1], (TOKENS, 2), jnp.float32, 0.1, 1.0), 0.1, 1.0)
    expert_ids = draw_expert_ids(jax.random.fold_in(keys[8], 71), 0)
    expert_counts = draw_expert_counts(jax.random.fold_in(keys[8], 71), 0)
    w_gate = noise(keys[4], (EXPERTS, D, FF), D ** -0.5, 0.078125, ((1, 4), (2, 8)))
    w_up = noise(keys[5], (EXPERTS, D, FF), D ** -0.5, 0.078125, ((1, 4), (2, 8)))
    w_down = noise(keys[6], (EXPERTS, FF, D), FF ** -0.5, 0.046875, ((1, 8), (2, 4)))
    cotangent = noise(keys[7], (TOKENS, D), 1.0, 6.0, ((0, 8), (1, 4)))
    return dict(tokens=tokens, combine=combine, expert_ids=expert_ids, expert_counts=expert_counts, w_gate=w_gate, w_up=w_up, w_down=w_down, cotangent=cotangent)


def route_layout(expert_ids, expert_counts, tokens_total, capacity):
    flat_ids = expert_ids.reshape(-1).astype(jnp.int32)
    onehot = (flat_ids[:, None] == jnp.arange(EXPERTS, dtype=jnp.int32)[None, :]).astype(jnp.int32)
    within = jnp.sum((jnp.cumsum(onehot, 0) - onehot) * onehot, 1)
    padded = (expert_counts.astype(jnp.int32) + BLOCK - 1) // BLOCK * BLOCK
    block_ends = jnp.cumsum(padded)
    block_starts = block_ends - padded
    slot_index = jnp.sum(onehot * block_starts[None, :], 1) + within
    entry_token = jnp.arange(flat_ids.shape[0], dtype=jnp.int32) // 2
    owner_token = jnp.full((capacity,), tokens_total, jnp.int32).at[slot_index].set(entry_token)
    first_rows = jnp.arange(capacity // BLOCK, dtype=jnp.int32) * BLOCK
    block_expert = jnp.minimum(jnp.sum((block_ends[None, :] <= first_rows[:, None]).astype(jnp.int32), 1), EXPERTS - 1)
    return slot_index, owner_token, block_expert


def blocked_product(rows, weights, block_expert, transpose):
    nblocks = block_expert.shape[0]
    blocks = rows.reshape(nblocks, rows.shape[0] // nblocks, rows.shape[1])

    def apply_block(operand):
        segment, expert = operand
        matrix = lax.dynamic_index_in_dim(weights, expert, 0, keepdims=False)
        if transpose:
            return lax.dot_general(segment, matrix, (((1,), (1,)), ((), ())), preferred_element_type=jnp.float32)
        return jnp.dot(segment, matrix, preferred_element_type=jnp.float32)

    result = lax.map(apply_block, (blocks, block_expert))
    return result.reshape(rows.shape[0], result.shape[2])


def reference(tokens, combine, expert_ids, expert_counts, w_gate, w_up, w_down, cotangent):
    tokens_total = tokens.shape[0]
    capacity = 2 * tokens_total + EXPERTS * BLOCK
    slot_index, owner_token, block_expert = route_layout(expert_ids, expert_counts, tokens_total, capacity)
    slot_pairs = slot_index.reshape(tokens_total, 2)
    zero_row = jnp.zeros((1, tokens.shape[1]), tokens.dtype)
    rows = jnp.concatenate([tokens, zero_row], 0)[owner_token]
    gate = blocked_product(rows, w_gate, block_expert, False)
    up = blocked_product(rows, w_up, block_expert, False)
    sigmoid = jax.nn.sigmoid(gate)
    active = gate * sigmoid
    hidden = (active * up).astype(jnp.bfloat16)
    out_rows = blocked_product(hidden, w_down, block_expert, False)
    layer_out = jnp.sum(combine[:, :, None] * out_rows[slot_pairs], 1).astype(jnp.bfloat16)
    combine_slot = jnp.zeros((capacity,), jnp.float32).at[slot_index].set(combine.reshape(-1))
    cot_rows = jnp.concatenate([cotangent, zero_row], 0)[owner_token].astype(jnp.float32)
    row_grad = (combine_slot[:, None] * cot_rows).astype(jnp.bfloat16)
    d_hidden = blocked_product(row_grad, w_down, block_expert, True)
    row_expert = jnp.repeat(block_expert, BLOCK)
    grads = []
    for expert in range(EXPERTS):
        chosen = jnp.where((row_expert == expert)[:, None], hidden, jnp.zeros_like(hidden))
        grads.append(lax.dot_general(chosen, row_grad, (((0,), (0,)), ((), ())), preferred_element_type=jnp.float32).astype(jnp.bfloat16))
    d_down = jnp.stack(grads, 0)
    d_gate = (d_hidden * up * sigmoid * (1.0 + gate * (1.0 - sigmoid))).astype(jnp.bfloat16)
    d_up = (d_hidden * active).astype(jnp.bfloat16)
    d_rows = blocked_product(d_gate, w_gate, block_expert, True) + blocked_product(d_up, w_up, block_expert, True)
    d_tokens = jnp.sum(d_rows[slot_pairs], 1).astype(jnp.bfloat16)
    return layer_out, d_tokens, d_down
```

```python
import functools

import jax
import jax.numpy as jnp
from jax import lax
from jax.experimental import pallas as pl
from jax.experimental.pallas import tpu as pltpu
from jax.sharding import PartitionSpec as P

SUB = 256
F32 = jnp.float32
BF16 = jnp.bfloat16
VMEM_LIMIT = 40 * 1024 * 1024


def dot(a, b, contract):
    return lax.dot_general(a, b, ((contract[0], contract[1]), ((), ())), preferred_element_type=F32)


def partial_kernel(masked, order, x, rg, other, wg, wu, wd, *rest):
    own, send = rest[-2:]
    step = pl.program_id(1)
    terms = (
        dot(x[...], wg[0], ((1,), (0,))),
        dot(x[...], wu[0], ((1,), (0,))),
        dot(rg[...], wd[0], ((1,), (1,))),
    )
    if not masked:
        for n, term in enumerate(terms):
            own[n] = term
            send[n] = term.astype(BF16)
        return
    chosen = other[...] == order[1 + step]
    last = pl.num_programs(1) - 1

    @pl.when(step == 0)
    def _():
        for n, term in enumerate(terms):
            own[n] = term

    @pl.when(step > 0)
    def _():
        for n, term in enumerate(terms):
            own[n] = jnp.where(chosen, term, own[n])

    @pl.when(step == last)
    def _():
        for n in range(3):
            send[n] = own[n].astype(BF16)


def partial_products(chunk, order, x, rg, other, w_gate, w_up, w_down, after):
    group, start, width = chunk
    experts, depth, _ = w_gate.shape
    rows = x.shape[0]
    sub = min(SUB, width)
    first, count = (0, 1) if group == 0 else (1, experts - 1)
    base = start // sub
    const = lambda j, e, order: (0, 0)
    column = lambda j, e, order: (order[first + e], 0, base + j)
    row = lambda j, e, order: (order[first + e], base + j, 0)
    out = lambda j, e, order: (0, 0, j)
    return pl.pallas_call(
        functools.partial(partial_kernel, group == 1),
        grid_spec=pltpu.PrefetchScalarGridSpec(
            num_scalar_prefetch=1,
            grid=(width // sub, count),
            in_specs=[
                pl.BlockSpec((rows, depth), const),
                pl.BlockSpec((rows, depth), const),
                pl.BlockSpec((rows, 1), const),
                pl.BlockSpec((1, depth, sub), column),
                pl.BlockSpec((1, depth, sub), column),
                pl.BlockSpec((1, sub, depth), row),
            ]
            + [pl.BlockSpec(memory_space=pl.ANY)] * len(after),
            out_specs=[
                pl.BlockSpec((3, rows, sub), out),
                pl.BlockSpec((3, rows, sub), out),
            ],
        ),
        out_shape=[
            jax.ShapeDtypeStruct((3, rows, width), F32),
            jax.ShapeDtypeStruct((3, rows, width), BF16),
        ],
        compiler_params=pltpu.CompilerParams(vmem_limit_bytes=VMEM_LIMIT),
        cost_estimate=pl.CostEstimate(
            flops=6 * rows * depth * width * count,
            bytes_accessed=6 * depth * width * count + 18 * rows * width,
            transcendentals=0,
        ),
        name="partial",
    )(order, x, rg, other, w_gate, w_up, w_down, *after)


def post_kernel(masked, opening, closing, order, mine, came, rg, weight, other, wg, wu, wd, *rest):
    picked, rest = rest[-1], rest[:-1]
    if not opening:
        sums_in, rest = rest[0], rest[2:]
    sums, d_down, pieces = rest[0], rest[1], rest[2:]
    j, step = pl.program_id(0), pl.program_id(1)

    @pl.when(jnp.logical_and(j == 0, step == 0))
    def _():
        sums[...] = jnp.zeros_like(sums) if opening else sums_in[...]

    edge = order[order.shape[0] - 1]

    @pl.when(jnp.logical_and(step == 0, edge == 1))
    def _():
        picked[...] = came[...]

    @pl.when(jnp.logical_and(step == 0, edge == 0))
    def _():
        picked[...] = mine[...]

    hidden, d_gate, d_up = picked[0], picked[1], picked[2]
    if masked:
        chosen = other[...] == order[1 + step]
        hidden = jnp.where(chosen, hidden, jnp.zeros_like(hidden))
        d_gate = jnp.where(chosen, d_gate, jnp.zeros_like(d_gate))
        d_up = jnp.where(chosen, d_up, jnp.zeros_like(d_up))
    sums[0] += weight[...] * dot(hidden, wd[0], ((1,), (0,)))
    sums[1] += dot(d_gate, wg[0], ((1,), (1,))) + dot(d_up, wu[0], ((1,), (1,)))
    d_down[0] = dot(hidden, rg[...], ((0,), (0,))).astype(BF16)

    if closing:

        @pl.when(jnp.logical_and(j == pl.num_programs(0) - 1, step == pl.num_programs(1) - 1))
        def _():
            size = pieces[0].shape[1]
            for n, piece in enumerate(pieces):
                piece[...] = sums[:, n * size : (n + 1) * size].astype(BF16)


def post_products(chunk, order, mine, came, rg, weight, other, w_gate, w_up, w_down, state, pieces):
    group, start, width = chunk
    experts, depth, units = w_gate.shape
    rows = rg.shape[0]
    sub = min(SUB, width)
    first, count = (0, 1) if group == 0 else (1, experts - 1)
    base = start // sub
    const = lambda j, e, order: (0, 0)
    whole = lambda j, e, order: (0, 0, 0)
    column = lambda j, e, order: (order[first + e], 0, base + j)
    row = lambda j, e, order: (order[first + e], base + j, 0)
    part = lambda j, e, order: (0, 0, j)
    opening = state is None
    sums_spec = pl.BlockSpec((2, rows, depth), whole)
    in_specs = [
        pl.BlockSpec((3, rows, sub), part),
        pl.BlockSpec((3, rows, sub), part),
        pl.BlockSpec((rows, depth), const),
        pl.BlockSpec((rows, 1), const),
        pl.BlockSpec((rows, 1), const),
        pl.BlockSpec((1, depth, sub), column),
        pl.BlockSpec((1, depth, sub), column),
        pl.BlockSpec((1, sub, depth), row),
    ]
    operands = [order, mine, came, rg, weight, other, w_gate, w_up, w_down]
    aliases = {}
    if not opening:
        in_specs += [sums_spec, pl.BlockSpec(memory_space=pl.ANY)]
        aliases = {len(operands): 0, len(operands) + 1: 1}
        operands += list(state)
    out_specs = [sums_spec, pl.BlockSpec((1, sub, depth), row)]
    out_shape = [
        jax.ShapeDtypeStruct((2, rows, depth), F32),
        jax.ShapeDtypeStruct((experts, units, depth), BF16),
    ]
    if pieces:
        out_specs += [pl.BlockSpec((2, rows // pieces, depth), whole)] * pieces
        out_shape += [jax.ShapeDtypeStruct((2, rows // pieces, depth), BF16)] * pieces
    return pl.pallas_call(
        functools.partial(post_kernel, group == 1, opening, pieces > 0),
        grid_spec=pltpu.PrefetchScalarGridSpec(
            num_scalar_prefetch=1,
            grid=(width // sub, count),
            in_specs=in_specs,
            out_specs=out_specs,
            scratch_shapes=[pltpu.VMEM((3, rows, sub), BF16)],
        ),
        out_shape=out_shape,
        input_output_aliases=aliases,
        compiler_params=pltpu.CompilerParams(vmem_limit_bytes=VMEM_LIMIT),
        cost_estimate=pl.CostEstimate(
            flops=8 * rows * depth * width * count,
            bytes_accessed=8 * depth * width * count + 16 * rows * depth,
            transcendentals=0,
        ),
        name="post",
    )(*operands)


def activations(gate, up, d_hidden):
    sigmoid = jax.nn.sigmoid(gate)
    active = gate * sigmoid
    hidden = (active * up).astype(BF16)
    d_gate = (d_hidden * up * sigmoid * (1.0 + gate * (1.0 - sigmoid))).astype(BF16)
    d_up = (d_hidden * active).astype(BF16)
    return jnp.stack([hidden, d_gate, d_up], 0)


def shift(x, step, size):
    return lax.ppermute(x, "tensor", [(i, (i - step) % size) for i in range(size)])


def chunk_plan(units):
    width = min(512, units)
    blocks = [(start, width) for start in range(0, units, width)]
    plan = [(0,) + blocks[0]]
    for n in range(len(blocks) - 1):
        plan += [(1,) + blocks[n], (0,) + blocks[n + 1]]
    plan = plan[:-1] + [(1,) + blocks[-1], plan[-1]] if len(blocks) > 1 else plan + [(1,) + blocks[-1]]
    return plan


def on_device(sections, parts, tokens, combine, expert_ids, expert_counts, w_gate, w_up, w_down, cotangent):
    total = combine.shape[0]
    local = tokens.shape[0]
    experts = w_gate.shape[0]
    me = lax.axis_index("tensor")
    place = lax.axis_index("section")

    x = jnp.concatenate([tokens] + [shift(tokens, n, parts) for n in range(1, parts)], 0)
    cot = jnp.concatenate([cotangent] + [shift(cotangent, n, parts) for n in range(1, parts)], 0)

    def turned(v):
        return lax.dynamic_slice_in_dim(jnp.concatenate([v, v], 0), me * local, total, 0)

    weights, ids = turned(combine), turned(expert_ids)
    common = jnp.argmax(expert_counts).astype(jnp.int32)
    ranks = jnp.arange(experts - 1, dtype=jnp.int32)
    line = sections == 4
    edge = jnp.logical_or(place == 0, place == sections - 1) if line else jnp.zeros((), bool)
    order = jnp.concatenate(
        [common[None], ranks + (ranks >= common).astype(jnp.int32), edge.astype(jnp.int32)[None]]
    )
    is_first = ids[:, :1] == common
    other = jnp.where(is_first, ids[:, 1:], ids[:, :1])
    weight = (
        jnp.where(is_first, weights[:, :1], weights[:, 1:]),
        jnp.where(is_first, weights[:, 1:], weights[:, :1]),
    )
    rg = tuple((w * cot.astype(F32)).astype(BF16) for w in weight)

    plan = chunk_plan(w_gate.shape[2])
    count = len(plan)
    own, sent, summed, mine, came = {}, {}, {}, {}, {}
    state = None

    def send(v, pairs):
        return lax.ppermute(v, "section", pairs)

    def begin(k, after):
        own[k], send_k = partial_products(
            plan[k], order, x, rg[plan[k][0]], other, w_gate, w_up, w_down, after
        )
        sent[k] = send(send_k, [(0, 1), (3, 2)]) if line else None

    def merge(k):
        if not line:
            return None
        summed[k] = own[k] + sent[k].astype(F32)
        packed = summed[k].astype(BF16)
        sent[k] = send(packed, [(1, 2), (2, 1)])
        return packed

    def finish(k):
        if line:
            full = summed[k] + sent[k].astype(F32)
            mine[k] = activations(full[0], full[1], full[2])
            came[k] = send(mine[k], [(1, 0), (2, 3)])
        else:
            full = lax.psum(own[k], "section")
            mine[k] = came[k] = activations(full[0], full[1], full[2])

    for k in range(2):
        begin(k, ())
    for step in range(count + 2):
        after = ()
        if step < count:
            packed = merge(step)
            after = () if packed is None else (packed,)
        if 1 <= step <= count:
            finish(step - 1)
        if step + 2 < count:
            begin(step + 2, after)
        if step >= 2:
            k = step - 2
            group = plan[k][0]
            state = post_products(
                plan[k], order, mine[k], came[k], rg[group], weight[group], other,
                w_gate, w_up, w_down, state, parts if k == count - 1 else 0,
            )
    d_down = state[1]
    pieces = state[2:]
    result = pieces[0].astype(F32)
    for n in range(1, parts):
        result += lax.ppermute(
            pieces[n], "tensor", [(i, (i + n) % parts) for i in range(parts)]
        ).astype(F32)
    result = result.astype(BF16)
    return result[0], result[1], d_down


def solution(mesh):
    in_specs = (
        P("tensor", "section"),
        P(),
        P(),
        P(),
        P(None, "section", "tensor"),
        P(None, "section", "tensor"),
        P(None, "tensor", "section"),
        P("tensor", "section"),
    )
    out_specs = (P("tensor", "section"), P("tensor", "section"), P(None, "tensor", "section"))
    return jax.shard_map(
        functools.partial(on_device, mesh.shape["section"], mesh.shape["tensor"]),
        mesh=mesh,
        in_specs=in_specs,
        out_specs=out_specs,
        check_vma=False,
    )
```

```python
import functools

import jax
import jax.numpy as jnp
import numpy as np
from jax import lax
from jax.experimental import pallas as pl
from jax.experimental.pallas import tpu as pltpu
from jax.sharding import PartitionSpec as P

SUB = 256
SLOTS = 4
F32 = jnp.float32
BF16 = jnp.bfloat16
COST_SCALE = 16
VMEM_LIMIT = 40 * 1024 * 1024
ANY = pl.BlockSpec(memory_space=pl.ANY)
VMEM = pl.BlockSpec(memory_space=pltpu.VMEM)
EXPERT, UNIT, GROUP, COLUMN, FIRST, LAST, FIELDS = 0, 1, 2, 3, 4, 5, 6


def dot(a, b, contract):
    return lax.dot_general(a, b, ((contract[0], contract[1]), ((), ())), preferred_element_type=F32)


def weight_copies(field, i, weights, buffers, sems):
    slot = lax.rem(i, SLOTS)
    expert = field(i, EXPERT)
    units = pl.ds(pl.multiple_of(field(i, COLUMN), SUB), SUB)
    wg, wu, wd = weights
    return (
        pltpu.make_async_copy(wg.at[expert, :, units], buffers[0].at[slot], sems.at[slot, 0]),
        pltpu.make_async_copy(wu.at[expert, :, units], buffers[1].at[slot], sems.at[slot, 1]),
        pltpu.make_async_copy(wd.at[expert, units, :], buffers[2].at[slot], sems.at[slot, 2]),
    )


def begin_all(copies):
    for copy in copies:
        copy.start()


def wait_all(copies):
    for copy in copies:
        copy.wait()


def partial_kernel(base, blocks, units, deps, table, other, x, rg, wg, wu, wd, *rest):
    own, send, zero, xv, rgv, b0, b1, b2, ownv, sendv, wsem, isem, osem = rest[deps:]
    zero[...] = jnp.zeros_like(zero)
    field = lambda i, n: table[(base + i) * FIELDS + n]
    fetch = lambda i: weight_copies(field, i, (wg, wu, wd), (b0, b1, b2), wsem)
    inputs = (pltpu.make_async_copy(x, xv, isem.at[0]), pltpu.make_async_copy(rg, rgv, isem.at[1]))
    inputs[0].start()
    begin_all(fetch(0))
    inputs[1].start()
    for i in range(1, min(SLOTS - 1, blocks)):
        begin_all(fetch(i))
    wait_all(inputs)

    def leave(unit):
        return (
            pltpu.make_async_copy(ownv.at[unit], own.at[unit], osem.at[unit, 0]),
            pltpu.make_async_copy(sendv.at[unit], send.at[unit], osem.at[unit, 1]),
        )

    def body(i, carry):
        @pl.when(i + (SLOTS - 1) < blocks)
        def _():
            begin_all(fetch(i + (SLOTS - 1)))

        wait_all(fetch(i))
        slot, unit, group = lax.rem(i, SLOTS), field(i, UNIT), field(i, GROUP)
        keep = jnp.logical_or(other[...] == field(i, EXPERT), field(i, FIRST) == 1)
        terms = (
            dot(xv[...], b0[slot], ((1,), (0,))),
            dot(xv[...], b1[slot], ((1,), (0,))),
            dot(rgv[group], b2[slot], ((1,), (1,))),
        )
        for n, term in enumerate(terms):
            ownv[unit, n] = jnp.where(keep, term, ownv[unit, n])

        @pl.when(field(i, LAST) == 1)
        def _():
            for n in range(3):
                sendv[unit, n] = ownv[unit, n].astype(BF16)
            begin_all(leave(unit))

        return carry

    lax.fori_loop(0, blocks, body, 0)
    for unit in range(units):
        wait_all(leave(unit))


def partial_products(base, blocks, units, table, x, rg, other, weights, after):
    experts, depth, _ = weights[0].shape
    rows = x.shape[0]
    shape = (units, 3, rows, SUB)
    return pl.pallas_call(
        functools.partial(partial_kernel, base, blocks, units, len(after)),
        grid_spec=pltpu.PrefetchScalarGridSpec(
            num_scalar_prefetch=1,
            grid=(),
            in_specs=[VMEM] + [ANY] * (5 + len(after)),
            out_specs=[ANY, ANY, VMEM],
            scratch_shapes=[
                pltpu.VMEM((rows, depth), BF16),
                pltpu.VMEM((2, rows, depth), BF16),
                pltpu.VMEM((SLOTS, depth, SUB), BF16),
                pltpu.VMEM((SLOTS, depth, SUB), BF16),
                pltpu.VMEM((SLOTS, SUB, depth), BF16),
                pltpu.VMEM(shape, F32),
                pltpu.VMEM(shape, BF16),
                pltpu.SemaphoreType.DMA((SLOTS, 3)),
                pltpu.SemaphoreType.DMA((2,)),
                pltpu.SemaphoreType.DMA((units, 2)),
            ],
        ),
        out_shape=[
            jax.ShapeDtypeStruct(shape, F32),
            jax.ShapeDtypeStruct(shape, BF16),
            jax.ShapeDtypeStruct((1, SUB), F32),
        ],
        compiler_params=pltpu.CompilerParams(vmem_limit_bytes=VMEM_LIMIT),
        cost_estimate=pl.CostEstimate(
            flops=6 * rows * depth * SUB * blocks // COST_SCALE,
            bytes_accessed=6 * depth * SUB * blocks // COST_SCALE,
            transcendentals=0,
        ),
        name="partial",
    )(table, other, x, rg, *weights, *after)


def post_kernel(base, blocks, units, deps, opening, closing, table, other, weight, mine, came, rg, wg, wu, wd, *rest):
    if not opening:
        sums_in, rest = rest[0], rest[2:]
    outs, scratch = rest[deps : deps + 3], rest[deps + 3 :]
    d_down = outs[0]
    if not closing:
        outs[2][...] = jnp.zeros_like(outs[2])
    act, rgv, b0, b1, b2, sums, ddv, wsem, isem, dsem = scratch
    field = lambda i, n: table[(base + i) * FIELDS + n]
    edge = table[table.shape[0] - 1]
    fetch = lambda i: weight_copies(field, i, (wg, wu, wd), (b0, b1, b2), wsem)
    take_mine = pltpu.make_async_copy(mine, act, isem.at[0])
    take_came = pltpu.make_async_copy(came, act, isem.at[0])
    take_rg = pltpu.make_async_copy(rg, rgv, isem.at[1])

    @pl.when(edge == 1)
    def _():
        take_came.start()

    @pl.when(edge == 0)
    def _():
        take_mine.start()

    begin_all(fetch(0))
    take_rg.start()
    if opening:
        sums[...] = jnp.zeros_like(sums)
    else:
        take_sums = pltpu.make_async_copy(sums_in, sums, isem.at[2])
        take_sums.start()
    for i in range(1, min(SLOTS - 1, blocks)):
        begin_all(fetch(i))
    take_mine.wait()
    take_rg.wait()
    if not opening:
        take_sums.wait()

    def leave(i):
        slot = lax.rem(i, 2)
        units = pl.ds(pl.multiple_of(field(i, COLUMN), SUB), SUB)
        return pltpu.make_async_copy(ddv.at[slot], d_down.at[field(i, EXPERT), units, :], dsem.at[slot])

    def body(i, carry):
        @pl.when(i + (SLOTS - 1) < blocks)
        def _():
            begin_all(fetch(i + (SLOTS - 1)))

        wait_all(fetch(i))

        @pl.when(i >= 2)
        def _():
            leave(i - 2).wait()

        slot, unit, group = lax.rem(i, SLOTS), field(i, UNIT), field(i, GROUP)
        keep = jnp.logical_or(other[...] == field(i, EXPERT), group == 0)
        hidden, d_gate, d_up = (
            jnp.where(keep, act[unit, n], jnp.zeros(act.shape[2:], BF16)) for n in range(3)
        )
        sums[0] += weight[group] * dot(hidden, b2[slot], ((1,), (0,)))
        sums[1] += dot(d_gate, b0[slot], ((1,), (1,))) + dot(d_up, b1[slot], ((1,), (1,)))
        ddv[lax.rem(i, 2)] = dot(hidden, rgv[group], ((0,), (0,))).astype(BF16)
        leave(i).start()
        return carry

    lax.fori_loop(0, blocks, body, 0)
    if closing:
        half = sums.shape[1] // 2
        outs[1][...] = sums[:, :half]
        outs[2][...] = sums[:, half:]
    else:
        put = pltpu.make_async_copy(sums, outs[1], isem.at[2])
        put.start()
    for i in range(max(blocks - 2, 0), blocks):
        leave(i).wait()
    if not closing:
        put.wait()


def post_products(base, blocks, units, table, mine, came, rg, weight, other, weights, state, after, closing):
    experts, depth, width = weights[0].shape
    rows = rg.shape[1]
    opening = state is None
    operands = [table, other, weight, mine, came, rg, *weights]
    in_specs = [VMEM, VMEM] + [ANY] * 6
    aliases = {}
    if not opening:
        aliases = {len(operands) + 1: 0}
        if not closing:
            aliases[len(operands)] = 1
        in_specs += [ANY, ANY]
        operands += [state[1], state[0]]
    in_specs += [ANY] * len(after)
    operands += list(after)
    out_shape = [jax.ShapeDtypeStruct((experts, width, depth), BF16)]
    out_specs = [ANY]
    if closing:
        out_shape += [jax.ShapeDtypeStruct((2, rows // 2, depth), F32)] * 2
        out_specs += [VMEM] * 2
    else:
        out_shape += [jax.ShapeDtypeStruct((2, rows, depth), F32), jax.ShapeDtypeStruct((1, SUB), F32)]
        out_specs += [ANY, VMEM]
    return pl.pallas_call(
        functools.partial(post_kernel, base, blocks, units, len(after), opening, closing),
        grid_spec=pltpu.PrefetchScalarGridSpec(
            num_scalar_prefetch=1,
            grid=(),
            in_specs=in_specs,
            out_specs=out_specs,
            scratch_shapes=[
                pltpu.VMEM((units, 3, rows, SUB), BF16),
                pltpu.VMEM((2, rows, depth), BF16),
                pltpu.VMEM((SLOTS, depth, SUB), BF16),
                pltpu.VMEM((SLOTS, depth, SUB), BF16),
                pltpu.VMEM((SLOTS, SUB, depth), BF16),
                pltpu.VMEM((2, rows, depth), F32),
                pltpu.VMEM((2, SUB, depth), BF16),
                pltpu.SemaphoreType.DMA((SLOTS, 3)),
                pltpu.SemaphoreType.DMA((3,)),
                pltpu.SemaphoreType.DMA((2,)),
            ],
        ),
        out_shape=out_shape,
        input_output_aliases=aliases,
        compiler_params=pltpu.CompilerParams(vmem_limit_bytes=VMEM_LIMIT),
        cost_estimate=pl.CostEstimate(
            flops=8 * rows * depth * SUB * blocks // COST_SCALE,
            bytes_accessed=8 * depth * SUB * blocks // COST_SCALE,
            transcendentals=0,
        ),
        name="post",
    )(*operands)


def activations(gate, up, d_hidden):
    sigmoid = jax.nn.sigmoid(gate)
    active = gate * sigmoid
    hidden = (active * up).astype(BF16)
    d_gate = (d_hidden * up * sigmoid * (1.0 + gate * (1.0 - sigmoid))).astype(BF16)
    d_up = (d_hidden * active).astype(BF16)
    return jnp.stack([hidden, d_gate, d_up], 1)


def chunk_plan(units):
    starts = list(range(0, units, SUB))
    first = [(0, s) for s in starts]
    second = [(1, s) for s in starts]
    if len(starts) < 8:
        return [[a, b] for a, b in zip(first, second)]
    head, tail, spare = first[:3], first[-2:], first[3:-2]
    plan = [head]
    groups = -(-len(second) // 2)
    for n in range(groups):
        extra = spare[n * len(spare) // (groups - 1) : (n + 1) * len(spare) // (groups - 1)] if n < groups - 1 else []
        plan.append(second[2 * n : 2 * n + 2] + extra)
    return plan + [tail]


def block_table(plan, experts):
    rows, spans = [], []
    for chunk in plan:
        base = len(rows)
        for unit, (group, start) in enumerate(chunk):
            ranks = [0] if group == 0 else list(range(1, experts))
            for rank in ranks:
                rows.append((rank, unit, group, start, int(rank == ranks[0]), int(rank == ranks[-1])))
        spans.append((base, len(rows) - base, len(chunk)))
    return np.array(rows, np.int32), spans


def sequence(count):
    steps = [("partial", k) for k in range(min(3, count))]
    for k in range(count + 2):
        if k < count and not (count == 6 and k == 5):
            steps.append(("merge", k))
        if 1 <= k <= count and not (count == 6 and k == 6):
            steps.append(("finish", k - 1))
        if count == 6 and k == 4:
            steps.append(("merge", 5))
        if count == 6 and k == 5:
            steps.append(("finish", 5))
        if k >= 2:
            steps.append(("post", k - 2))
        if k + 3 < count:
            steps.append(("partial", k + 3))
    return steps


def on_device(sections, parts, tokens, combine, expert_ids, expert_counts, w_gate, w_up, w_down, cotangent):
    total = combine.shape[0]
    local = tokens.shape[0]
    experts = w_gate.shape[0]
    weights = (w_gate, w_up, w_down)
    chips = parts // 2
    me = lax.axis_index("tensor")
    place = lax.axis_index("section")
    chip, core = me // 2, me % 2

    pair = jnp.stack([tokens, cotangent], 0)
    near = jnp.concatenate(
        [pair]
        + [lax.ppermute(pair, "tensor", [(i, (i - 2 * n) % parts) for i in range(parts)]) for n in range(1, chips)],
        1,
    )
    swap = [(i, i ^ 1) for i in range(parts)]
    far = lax.ppermute(near, "tensor", swap)
    full = jnp.concatenate([near, far], 1)
    x, cot = full[0], full[1]

    def turned(v):
        v = v.reshape(chips, 2, local, v.shape[1])
        v = jnp.where(core == 1, v[:, ::-1], v).transpose(1, 0, 2, 3)
        v = lax.dynamic_slice_in_dim(jnp.concatenate([v, v], 1), chip, chips, 1)
        return v.reshape(total, v.shape[3])

    scale, ids = turned(combine), turned(expert_ids)
    common = jnp.argmax(expert_counts).astype(jnp.int32)
    is_first = ids[:, :1] == common
    other = jnp.where(is_first, ids[:, 1:], ids[:, :1])
    weight = jnp.stack(
        [
            jnp.where(is_first, scale[:, :1], scale[:, 1:]),
            jnp.where(is_first, scale[:, 1:], scale[:, :1]),
        ],
        0,
    )
    rg = (weight * cot.astype(F32)[None]).astype(BF16)

    plan = chunk_plan(w_gate.shape[2])
    rows, spans = block_table(plan, experts)
    line = sections == 4
    edge = jnp.logical_or(place == 0, place == sections - 1) if line else jnp.zeros((), bool)
    rank = jnp.asarray(rows[:, EXPERT])
    expert = jnp.where(rank == 0, common, rank - (rank <= common).astype(jnp.int32))
    table = jnp.concatenate([expert[:, None], jnp.asarray(rows[:, 1:])], 1).reshape(-1)
    table = jnp.concatenate([table, edge.astype(jnp.int32)[None]])

    count = len(plan)
    own, sent, summed, mine, came = {}, {}, {}, {}, {}
    state = None
    after = ()

    def send(v, pairs):
        return lax.ppermute(v, "section", pairs)

    for name, k in sequence(count):
        if name == "partial":
            own[k], packed, zero = partial_products(*spans[k], table, x, rg, other, weights, after)
            sent[k] = send(packed, [(0, 1), (3, 2)]) if line else None
            after = (zero,)
        elif name == "merge" and line:
            summed[k] = own[k] + (sent[k].astype(F32) + zero)
            packed = summed[k].astype(BF16)
            sent[k] = send(packed, [(1, 2), (2, 1)])
            after += (packed,)
        elif name == "finish" and line:
            all_of = summed[k] + (sent[k].astype(F32) + zero)
            mine[k] = activations(all_of[:, 0], all_of[:, 1], all_of[:, 2])
            came[k] = send(mine[k], [(1, 0), (2, 3)])
            after += (mine[k],)
        elif name == "finish":
            all_of = lax.psum(own[k], "section")
            mine[k] = came[k] = activations(all_of[:, 0], all_of[:, 1], all_of[:, 2])
        elif name == "post":
            *state, zero = post_products(
                *spans[k], table, mine[k], came[k], rg, weight, other, weights, state, after, k == count - 1
            )
            after = (zero,)
    (d_down, keep), give = state, zero
    both = keep + lax.ppermute(give, "tensor", swap)
    result = both[:, :local]
    for n in range(1, chips):
        piece = both[:, n * local : (n + 1) * local].astype(BF16)
        result += lax.ppermute(piece, "tensor", [(i, (i + 2 * n) % parts) for i in range(parts)]).astype(F32)
    return result[0].astype(BF16), result[1].astype(BF16), d_down


def solution(mesh):
    in_specs = (
        P("tensor", "section"),
        P(),
        P(),
        P(),
        P(None, "section", "tensor"),
        P(None, "section", "tensor"),
        P(None, "tensor", "section"),
        P("tensor", "section"),
    )
    out_specs = (P("tensor", "section"), P("tensor", "section"), P(None, "tensor", "section"))
    return jax.shard_map(
        functools.partial(on_device, mesh.shape["section"], mesh.shape["tensor"]),
        mesh=mesh,
        in_specs=in_specs,
        out_specs=out_specs,
        check_vma=False,
    )
```

```python
import functools

import jax
import jax.numpy as jnp
from jax import lax
from jax.experimental import pallas as pl
from jax.experimental.pallas import tpu as pltpu
from jax.sharding import PartitionSpec as P

SUB = 512
EARLY = 2
SLOTS = EARLY + 1
F32 = jnp.float32
BF16 = jnp.bfloat16
COST_SCALE = 1
VMEM_LIMIT = 20 * 1024 * 1024
ANY = pl.BlockSpec(memory_space=pl.ANY)
HBM = pl.BlockSpec(memory_space=pltpu.HBM)
VMEM = pl.BlockSpec(memory_space=pltpu.VMEM)
EXPERT, UNIT, GROUP, COLUMN, FIRST, LAST, FIELDS = 0, 1, 2, 3, 4, 5, 6


def dot(a, b, contract):
    return lax.dot_general(a, b, ((contract[0], contract[1]), ((), ())), preferred_element_type=F32)


def fill_table(rows, base, head, table):
    order = {rank: head[0, rank] for rank in sorted({row[EXPERT] for row in rows})}
    for n, row in enumerate(rows):
        for field, value in enumerate(row):
            table[n * FIELDS + field] = order[value] if field == EXPERT else value
    return lambda i, field: table[(i - base) * FIELDS + field]


def weight_copies(field, i, weights, buffers, sems):
    slot = lax.rem(i, SLOTS)
    expert = field(i, EXPERT)
    units = pl.ds(pl.multiple_of(field(i, COLUMN), SUB), SUB)
    wg, wu, wd = weights
    return (
        pltpu.make_async_copy(wg.at[expert, :, units], buffers[0].at[slot], sems.at[slot, 0]),
        pltpu.make_async_copy(wu.at[expert, :, units], buffers[1].at[slot], sems.at[slot, 1]),
        pltpu.make_async_copy(wd.at[expert, units, :], buffers[2].at[slot], sems.at[slot, 2]),
    )


def over_blocks(span, total, fetch, work):
    base, end = span
    if base == 0:
        for i in range(min(EARLY, total)):
            begin_all(fetch(i))
    loaded = 0 if base == 0 else base + EARLY

    def body(i, carry):
        @pl.when(i + EARLY < total)
        def _():
            begin_all(fetch(i + EARLY))

        @pl.when(i >= loaded)
        def _():
            wait_all(fetch(i))

        work(i)
        return carry

    lax.fori_loop(base, end, body, 0)
    for i in range(max(end, loaded), min(end + EARLY, total)):
        wait_all(fetch(i))


def begin_all(copies):
    for copy in copies:
        copy.start()


def wait_all(copies):
    for copy in copies:
        copy.wait()


def partial_kernel(span, total, rows, first, deps, head, other, x, rg, wg, wu, wd, *rest):
    b0, b1, b2, own, send, zero, table, wsem = rest[deps + (0 if first else 3) :]
    field = fill_table(rows, span[0], head, table)
    fetch = lambda i: weight_copies(field, i, (wg, wu, wd), (b0, b1, b2), wsem)
    zero[...] = jnp.zeros_like(zero)

    def work(i):
        slot, unit, group = lax.rem(i, SLOTS), field(i, UNIT), field(i, GROUP)
        keep = jnp.logical_or(other[...] == field(i, EXPERT), field(i, FIRST) == 1)
        terms = (
            dot(x[...], b0[slot], ((1,), (0,))),
            dot(x[...], b1[slot], ((1,), (0,))),
            dot(rg[group], b2[slot], ((1,), (1,))),
        )
        for n, term in enumerate(terms):
            own[unit, n] = jnp.where(keep, term, own[unit, n])

        @pl.when(field(i, LAST) == 1)
        def _():
            for n in range(3):
                send[unit, n] = own[unit, n].astype(BF16)

    over_blocks(span, total, fetch, work)


def near_core(v):
    return pltpu.with_memory_space_constraint(v, pltpu.VMEM)


def slot_shapes(depth):
    return [pltpu.VMEM((SLOTS, depth, SUB), BF16)] * 2 + [pltpu.VMEM((SLOTS, SUB, depth), BF16)]


def in_hbm(v):
    return pltpu.with_memory_space_constraint(v, pltpu.HBM)


def cost(products, rows, depth, blocks):
    return pl.CostEstimate(
        flops=int(2 * products * rows * depth * SUB * blocks / COST_SCALE),
        bytes_accessed=int(6 * depth * SUB * blocks / COST_SCALE),
        transcendentals=0,
    )


def partial_products(span, units, blocks, head, x, rg, other, weights, slots, after):
    depth = weights[0].shape[1]
    rows = x.shape[0]
    shape = (units, 3, rows, SUB)
    first = slots is None
    seen = blocks[span[0] : span[1] + EARLY]
    operands = [near_core(v) for v in (head, other, x, rg)] + [in_hbm(w) for w in weights] + list(after)
    in_specs = [VMEM] * 4 + [HBM] * 3 + [ANY] * len(after)
    aliases = {}
    if not first:
        aliases = {len(operands) + n: n for n in range(3)}
        operands += [near_core(v) for v in slots]
        in_specs += [VMEM] * 3
    out = pl.pallas_call(
        functools.partial(partial_kernel, span, len(blocks), seen, first, len(after)),
        in_specs=in_specs,
        out_specs=[VMEM] * 6,
        scratch_shapes=[pltpu.SMEM((len(seen) * FIELDS,), jnp.int32), pltpu.SemaphoreType.DMA((SLOTS, 3))],
        out_shape=slot_shapes(depth) + [pltpu.VMEM(shape, F32), pltpu.VMEM(shape, BF16), pltpu.VMEM((2, 1, SUB), F32)],
        input_output_aliases=aliases,
        compiler_params=pltpu.CompilerParams(vmem_limit_bytes=VMEM_LIMIT),
        cost_estimate=cost(3, rows, depth, span[1] - span[0]),
        name="partial",
    )(*operands)
    return out[:3], out[3], out[4], out[5]


def post_kernel(span, total, rows, deps, opening, closing, head, other, weight, mine, came, rg, wg, wu, wd, *rest):
    rest = rest[deps + 3 :]
    if not opening:
        sums_in, rest = rest[0], rest[2:]
    b0, b1, b2, d_down, sums, extra = rest[:6]
    ddv, table, wsem, dsem = rest[-4:]
    base, end = span
    field = fill_table(rows, base, head, table)
    edge = head[0, head.shape[1] - 1]
    fetch = lambda i: weight_copies(field, i, (wg, wu, wd), (b0, b1, b2), wsem)
    if closing:
        give, sums = sums, rest[6]
        sums[...] = jnp.zeros_like(sums) if opening else sums_in[...]
    else:
        extra[...] = jnp.zeros_like(extra)
        if opening:
            sums[...] = jnp.zeros_like(sums)

    def leave(i):
        slot = lax.rem(i, 2)
        units = pl.ds(pl.multiple_of(field(i, COLUMN), SUB), SUB)
        return pltpu.make_async_copy(ddv.at[slot], d_down.at[field(i, EXPERT), units, :], dsem.at[slot])

    def work(i):
        @pl.when(i >= base + 2)
        def _():
            leave(i - 2).wait()

        slot, unit, group = lax.rem(i, SLOTS), field(i, UNIT), field(i, GROUP)
        keep = jnp.logical_or(other[...] == field(i, EXPERT), group == 0)
        use_came = jnp.logical_and(keep, edge == 1)
        use_mine = jnp.logical_and(keep, edge == 0)
        hidden, d_gate, d_up = (
            jnp.where(use_came, came[unit, n], jnp.where(use_mine, mine[unit, n], jnp.zeros(mine.shape[2:], BF16)))
            for n in range(3)
        )
        ddv[lax.rem(i, 2)] = dot(hidden, rg[group], ((0,), (0,))).astype(BF16)
        leave(i).start()
        sums[0] += weight[group] * dot(hidden, b2[slot], ((1,), (0,)))
        sums[1] += dot(d_gate, b0[slot], ((1,), (1,))) + dot(d_up, b1[slot], ((1,), (1,)))

    over_blocks(span, total, fetch, work)
    if closing:
        half = sums.shape[1] // 2
        give[...] = sums[:, half:]
        extra[...] = sums[:, :half]
    for i in range(max(end - 2, base), end):
        leave(i).wait()


def post_products(span, blocks, head, mine, came, rg, weight, other, weights, slots, state, after, closing):
    experts, depth, width = weights[0].shape
    rows = rg.shape[1]
    opening = state is None
    seen = blocks[span[0] : span[1] + EARLY]
    operands = [near_core(v) for v in (head, other, weight, mine, came, rg)] + [in_hbm(w) for w in weights]
    operands += list(after)
    in_specs = [VMEM] * 6 + [HBM] * 3 + [ANY] * len(after) + [VMEM] * 3
    aliases = {len(operands) + n: n for n in range(3)}
    operands += [near_core(v) for v in slots]
    if not opening:
        aliases[len(operands) + 1] = 3
        if not closing:
            aliases[len(operands)] = 4
        in_specs += [VMEM, HBM]
        operands += [near_core(state[1]), in_hbm(state[0])]
    sums_shape = pltpu.VMEM((2, rows, depth), F32)
    out_shape = slot_shapes(depth) + [pltpu.HBM((experts, width, depth), BF16)]
    if closing:
        out_shape += [pltpu.VMEM((2, rows // 2, depth), F32)] * 2
    else:
        out_shape += [sums_shape, pltpu.VMEM((2, 1, SUB), F32)]
    out = pl.pallas_call(
        functools.partial(post_kernel, span, len(blocks), seen, len(after), opening, closing),
        in_specs=in_specs,
        out_specs=[VMEM] * 3 + [HBM, VMEM, VMEM],
        scratch_shapes=([sums_shape] if closing else [])
        + [
            pltpu.VMEM((2, SUB, depth), BF16),
            pltpu.SMEM((len(seen) * FIELDS,), jnp.int32),
            pltpu.SemaphoreType.DMA((SLOTS, 3)),
            pltpu.SemaphoreType.DMA((2,)),
        ],
        out_shape=out_shape,
        input_output_aliases=aliases,
        compiler_params=pltpu.CompilerParams(vmem_limit_bytes=VMEM_LIMIT),
        cost_estimate=cost(4, rows, depth, span[1] - span[0]),
        name="post",
    )(*operands)
    return out[:3], (out[3], out[4]), out[5]


def activations(gate, up, d_hidden):
    sigmoid = jax.nn.sigmoid(gate)
    active = gate * sigmoid
    hidden = (active * up).astype(BF16)
    d_gate = (d_hidden * up * sigmoid * (1.0 + gate * (1.0 - sigmoid))).astype(BF16)
    d_up = (d_hidden * active).astype(BF16)
    return jnp.stack([hidden, d_gate, d_up], 1)


def chunk_plan(units):
    starts = list(range(0, units, SUB))
    one, two = [[(0, s)] for s in starts], [[(1, s)] for s in starts]
    return one[:1] + two + one[1:]


def block_table(plan, steps, experts):
    rows, spans = [], {}
    for name, k in steps:
        if name not in ("partial", "post"):
            continue
        base = len(rows)
        for unit, (group, start) in enumerate(plan[k]):
            ranks = [0] if group == 0 else list(range(1, experts))
            for rank in ranks:
                rows.append((rank, unit, group, start, int(rank == ranks[0]), int(rank == ranks[-1])))
        spans[name, k] = (base, len(rows))
    return rows, spans


def sequence(count):
    if count != 8:
        return [(name, k) for k in range(count) for name in ("partial", "merge", "finish", "post")]
    return [(STEPS[word[0]], int(word[1:])) for word in ORDER]


STEPS = {"P": "partial", "M": "merge", "F": "finish", "Q": "post"}
ORDER = (
    "P0", "P1", "P2", "M0", "P3", "M1", "F0", "P4", "M2", "F1", "P5", "Q0",
    "M3", "F2", "Q1", "M4", "F3", "P6", "M5", "P7", "F4", "Q2", "M6", "F5",
    "Q3", "M7", "F6", "Q4", "Q5", "F7", "Q6", "Q7",
)


def on_device(sections, parts, tokens, combine, expert_ids, expert_counts, w_gate, w_up, w_down, cotangent):
    total = combine.shape[0]
    local = tokens.shape[0]
    experts = w_gate.shape[0]
    weights = (w_gate, w_up, w_down)
    chips = parts // 2
    me = lax.axis_index("tensor")
    place = lax.axis_index("section")
    chip, core = me // 2, me % 2

    pair = jnp.stack([tokens, cotangent], 0)
    near = jnp.concatenate(
        [pair]
        + [lax.ppermute(pair, "tensor", [(i, (i - 2 * n) % parts) for i in range(parts)]) for n in range(1, chips)],
        1,
    )
    swap = [(i, i ^ 1) for i in range(parts)]
    far = lax.ppermute(near, "tensor", swap)
    full = jnp.concatenate([near, far], 1)
    x, cot = full[0], full[1]

    def turned(v):
        v = v.reshape(chips, 2, local, v.shape[1])
        v = jnp.where(core == 1, v[:, ::-1], v).transpose(1, 0, 2, 3)
        v = lax.dynamic_slice_in_dim(jnp.concatenate([v, v], 1), chip, chips, 1)
        return v.reshape(total, v.shape[3])

    scale, ids = turned(combine), turned(expert_ids)
    common = jnp.argmax(expert_counts).astype(jnp.int32)
    is_first = ids[:, :1] == common
    other = jnp.where(is_first, ids[:, 1:], ids[:, :1])
    weight = jnp.stack(
        [
            jnp.where(is_first, scale[:, :1], scale[:, 1:]),
            jnp.where(is_first, scale[:, 1:], scale[:, :1]),
        ],
        0,
    )
    rg = (weight * cot.astype(F32)[None]).astype(BF16)

    plan = chunk_plan(w_gate.shape[2])
    count = len(plan)
    steps = sequence(count)
    blocks, spans = block_table(plan, steps, experts)
    line = sections == 4
    edge = jnp.logical_or(place == 0, place == sections - 1) if line else jnp.zeros((), bool)
    lane = jnp.arange(128, dtype=jnp.int32)
    head = jnp.where(lane == 0, common, lane - (lane <= common).astype(jnp.int32))
    head = jnp.where(lane == 127, edge.astype(jnp.int32), head)[None]

    own, sent, summed, mine, came = {}, {}, {}, {}, {}
    state = slots = None
    after = ()

    def send(v, pairs):
        return lax.ppermute(v, "section", pairs)

    for name, k in steps:
        if name == "partial":
            slots, own[k], packed, zero = partial_products(
                spans[name, k], len(plan[k]), blocks, head, x, rg, other, weights, slots, after
            )
            sent[k] = send(packed, [(0, 1), (3, 2)]) if line else None
            after = (zero,)
        elif name == "merge" and line:
            summed[k] = own[k] + (sent[k].astype(F32) + zero[0])
            packed = summed[k].astype(BF16)
            sent[k] = send(packed, [(1, 2), (2, 1)])
            after += (packed,)
        elif name == "finish" and line:
            all_of = summed[k] + (sent[k].astype(F32) + zero[1])
            mine[k] = activations(all_of[:, 0], all_of[:, 1], all_of[:, 2])
            came[k] = send(mine[k], [(1, 0), (2, 3)])
            after += (mine[k],)
        elif name == "finish":
            all_of = lax.psum(own[k], "section")
            mine[k] = came[k] = activations(all_of[:, 0], all_of[:, 1], all_of[:, 2])
        elif name == "post":
            slots, state, zero = post_products(
                spans[name, k], blocks, head, mine[k], came[k], rg, weight, other, weights, slots, state,
                after, k == count - 1,
            )
            after = (zero,)
    (d_down, give), keep = state, zero
    both = keep + lax.ppermute(give, "tensor", swap)
    result = both[:, :local]
    for n in range(1, chips):
        piece = both[:, n * local : (n + 1) * local].astype(BF16)
        result += lax.ppermute(piece, "tensor", [(i, (i + 2 * n) % parts) for i in range(parts)]).astype(F32)
    return result[0].astype(BF16), result[1].astype(BF16), d_down


def solution(mesh):
    in_specs = (
        P("tensor", "section"),
        P(),
        P(),
        P(),
        P(None, "section", "tensor"),
        P(None, "section", "tensor"),
        P(None, "tensor", "section"),
        P("tensor", "section"),
    )
    out_specs = (P("tensor", "section"), P("tensor", "section"), P(None, "tensor", "section"))
    return jax.shard_map(
        functools.partial(on_device, mesh.shape["section"], mesh.shape["tensor"]),
        mesh=mesh,
        in_specs=in_specs,
        out_specs=out_specs,
        check_vma=False,
    )
```

```python
import functools

import jax
import jax.numpy as jnp
from jax import lax
from jax.experimental import pallas as pl
from jax.experimental.pallas import tpu as pltpu
from jax.sharding import PartitionSpec as P

SUB = 512
EARLY = 2
SLOTS = EARLY + 1
F32 = jnp.float32
BF16 = jnp.bfloat16
COST_FACTOR = 4.0
VMEM_LIMIT = 20 * 1024 * 1024
ANY = pl.BlockSpec(memory_space=pl.ANY)
HBM = pl.BlockSpec(memory_space=pltpu.HBM)
VMEM = pl.BlockSpec(memory_space=pltpu.VMEM)
EXPERT, UNIT, GROUP, COLUMN, FIRST, LAST, FIELDS = 0, 1, 2, 3, 4, 5, 6


def dot(a, b, contract):
    return lax.dot_general(a, b, ((contract[0], contract[1]), ((), ())), preferred_element_type=F32)


def fill_table(rows, base, head, table):
    order = {rank: head[0, rank] for rank in sorted({row[EXPERT] for row in rows})}
    for n, row in enumerate(rows):
        for field, value in enumerate(row):
            table[n * FIELDS + field] = order[value] if field == EXPERT else value
    return lambda i, field: table[(i - base) * FIELDS + field]


def weight_copies(field, i, weights, buffers, sems):
    slot = lax.rem(i, SLOTS)
    expert = field(i, EXPERT)
    units = pl.ds(pl.multiple_of(field(i, COLUMN), SUB), SUB)
    wg, wu, wd = weights
    return (
        pltpu.make_async_copy(wg.at[expert, :, units], buffers[0].at[slot], sems.at[slot, 0]),
        pltpu.make_async_copy(wu.at[expert, :, units], buffers[1].at[slot], sems.at[slot, 1]),
        pltpu.make_async_copy(wd.at[expert, units, :], buffers[2].at[slot], sems.at[slot, 2]),
    )


def begin_all(copies):
    for copy in copies:
        copy.start()


def wait_all(copies):
    for copy in copies:
        copy.wait()


def preload_kernel(rows, head, wg, wu, wd, b0, b1, b2, table, wsem):
    field = fill_table(rows, 0, head, table)
    copies = [weight_copies(field, i, (wg, wu, wd), (b0, b1, b2), wsem) for i in range(len(rows))]
    for copy in copies:
        begin_all(copy)
    for copy in copies:
        wait_all(copy)


def over_blocks(span, total, fetch, work):
    base, end = span

    def body(i, carry):
        @pl.when(i + EARLY < total)
        def _():
            begin_all(fetch(i + EARLY))

        @pl.when(i >= base + EARLY)
        def _():
            wait_all(fetch(i))

        work(i)
        return carry

    lax.fori_loop(base, end, body, 0)
    for i in range(max(end, base + EARLY), min(end + EARLY, total)):
        wait_all(fetch(i))


def partial_kernel(span, total, rows, deps, head, other, x, rg, wg, wu, wd, *rest):
    b0, b1, b2, own, send, zero, table, wsem = rest[deps + 3 :]
    field = fill_table(rows, span[0], head, table)
    fetch = lambda i: weight_copies(field, i, (wg, wu, wd), (b0, b1, b2), wsem)
    zero[...] = jnp.zeros_like(zero)

    def work(i):
        slot, unit, group = lax.rem(i, SLOTS), field(i, UNIT), field(i, GROUP)
        keep = jnp.logical_or(other[...] == field(i, EXPERT), field(i, FIRST) == 1)
        terms = (
            dot(x[...], b0[slot], ((1,), (0,))),
            dot(x[...], b1[slot], ((1,), (0,))),
            dot(rg[group], b2[slot], ((1,), (1,))),
        )
        for n, term in enumerate(terms):
            own[unit, n] = jnp.where(keep, term, own[unit, n])

        @pl.when(field(i, LAST) == 1)
        def _():
            for n in range(3):
                send[unit, n] = own[unit, n].astype(BF16)

    over_blocks(span, total, fetch, work)


def near_core(v):
    return pltpu.with_memory_space_constraint(v, pltpu.VMEM)


def slot_shapes(depth):
    return [pltpu.VMEM((SLOTS, depth, SUB), BF16)] * 2 + [pltpu.VMEM((SLOTS, SUB, depth), BF16)]


def in_hbm(v):
    return pltpu.with_memory_space_constraint(v, pltpu.HBM)


def cost(products, rows, depth, blocks):
    return pl.CostEstimate(
        flops=int(2 * products * rows * depth * SUB * blocks * COST_FACTOR),
        bytes_accessed=int(6 * depth * SUB * blocks * COST_FACTOR),
        transcendentals=0,
    )


def preload(blocks, head, weights):
    depth = weights[0].shape[1]
    return pl.pallas_call(
        functools.partial(preload_kernel, blocks[:EARLY]),
        in_specs=[VMEM] + [HBM] * 3,
        out_specs=[VMEM] * 3,
        out_shape=slot_shapes(depth),
        scratch_shapes=[pltpu.SMEM((EARLY * FIELDS,), jnp.int32), pltpu.SemaphoreType.DMA((SLOTS, 3))],
        compiler_params=pltpu.CompilerParams(vmem_limit_bytes=VMEM_LIMIT),
        cost_estimate=cost(0, 0, depth, EARLY),
        name="preload",
    )(near_core(head), *[in_hbm(w) for w in weights])


def partial_products(span, units, blocks, head, x, rg, other, weights, slots, after):
    depth = weights[0].shape[1]
    rows = x.shape[0]
    shape = (units, 3, rows, SUB)
    seen = blocks[span[0] : span[1] + EARLY]
    operands = [near_core(v) for v in (head, other, x, rg)] + [in_hbm(w) for w in weights] + list(after)
    in_specs = [VMEM] * 4 + [HBM] * 3 + [ANY] * len(after) + [VMEM] * 3
    aliases = {len(operands) + n: n for n in range(3)}
    operands += [near_core(v) for v in slots]
    out = pl.pallas_call(
        functools.partial(partial_kernel, span, len(blocks), seen, len(after)),
        in_specs=in_specs,
        out_specs=[VMEM] * 6,
        scratch_shapes=[pltpu.SMEM((len(seen) * FIELDS,), jnp.int32), pltpu.SemaphoreType.DMA((SLOTS, 3))],
        out_shape=slot_shapes(depth) + [pltpu.VMEM(shape, F32), pltpu.VMEM(shape, BF16), pltpu.VMEM((2, 1, SUB), F32)],
        input_output_aliases=aliases,
        compiler_params=pltpu.CompilerParams(vmem_limit_bytes=VMEM_LIMIT),
        cost_estimate=cost(3, rows, depth, span[1] - span[0]),
        name="partial",
    )(*operands)
    return out[:3], out[3], out[4], out[5]


def post_kernel(span, total, rows, deps, opening, closing, head, other, weight, mine, came, rg, wg, wu, wd, *rest):
    rest = rest[deps + 3 :]
    if not opening:
        sums_in, rest = rest[0], rest[2:]
    b0, b1, b2, d_down, sums, extra = rest[:6]
    ddv, table, wsem, dsem = rest[-4:]
    base, end = span
    field = fill_table(rows, base, head, table)
    edge = head[0, head.shape[1] - 1]
    fetch = lambda i: weight_copies(field, i, (wg, wu, wd), (b0, b1, b2), wsem)
    if closing:
        give, sums = sums, rest[6]
        sums[...] = jnp.zeros_like(sums) if opening else sums_in[...]
    else:
        extra[...] = jnp.zeros_like(extra)
        if opening:
            sums[...] = jnp.zeros_like(sums)

    def leave(i):
        slot = lax.rem(i, 2)
        units = pl.ds(pl.multiple_of(field(i, COLUMN), SUB), SUB)
        return pltpu.make_async_copy(ddv.at[slot], d_down.at[field(i, EXPERT), units, :], dsem.at[slot])

    def work(i):
        @pl.when(i >= base + 2)
        def _():
            leave(i - 2).wait()

        slot, unit, group = lax.rem(i, SLOTS), field(i, UNIT), field(i, GROUP)
        keep = jnp.logical_or(other[...] == field(i, EXPERT), group == 0)
        use_came = jnp.logical_and(keep, edge == 1)
        use_mine = jnp.logical_and(keep, edge == 0)
        hidden, d_gate, d_up = (
            jnp.where(use_came, came[unit, n], jnp.where(use_mine, mine[unit, n], jnp.zeros(mine.shape[2:], BF16)))
            for n in range(3)
        )
        ddv[lax.rem(i, 2)] = dot(hidden, rg[group], ((0,), (0,))).astype(BF16)
        leave(i).start()
        sums[0] += weight[group] * dot(hidden, b2[slot], ((1,), (0,)))
        sums[1] += dot(d_gate, b0[slot], ((1,), (1,))) + dot(d_up, b1[slot], ((1,), (1,)))

    over_blocks(span, total, fetch, work)
    if closing:
        half = sums.shape[1] // 2
        give[...] = sums[:, half:].astype(BF16)
        extra[...] = sums[:, :half]
    for i in range(max(end - 2, base), end):
        leave(i).wait()


def post_products(span, blocks, head, mine, came, rg, weight, other, weights, slots, state, after, closing):
    experts, depth, width = weights[0].shape
    rows = rg.shape[1]
    opening = state is None
    seen = blocks[span[0] : span[1] + EARLY]
    operands = [near_core(v) for v in (head, other, weight, mine, came, rg)] + [in_hbm(w) for w in weights]
    operands += list(after)
    in_specs = [VMEM] * 6 + [HBM] * 3 + [ANY] * len(after) + [VMEM] * 3
    aliases = {len(operands) + n: n for n in range(3)}
    operands += [near_core(v) for v in slots]
    if not opening:
        aliases[len(operands) + 1] = 3
        if not closing:
            aliases[len(operands)] = 4
        in_specs += [VMEM, HBM]
        operands += [near_core(state[1]), in_hbm(state[0])]
    sums_shape = pltpu.VMEM((2, rows, depth), F32)
    out_shape = slot_shapes(depth) + [pltpu.HBM((experts, width, depth), BF16)]
    if closing:
        out_shape += [pltpu.VMEM((2, rows // 2, depth), kind) for kind in (BF16, F32)]
    else:
        out_shape += [sums_shape, pltpu.VMEM((2, 1, SUB), F32)]
    out = pl.pallas_call(
        functools.partial(post_kernel, span, len(blocks), seen, len(after), opening, closing),
        in_specs=in_specs,
        out_specs=[VMEM] * 3 + [HBM, VMEM, VMEM],
        scratch_shapes=([sums_shape] if closing else [])
        + [
            pltpu.VMEM((2, SUB, depth), BF16),
            pltpu.SMEM((len(seen) * FIELDS,), jnp.int32),
            pltpu.SemaphoreType.DMA((SLOTS, 3)),
            pltpu.SemaphoreType.DMA((2,)),
        ],
        out_shape=out_shape,
        input_output_aliases=aliases,
        compiler_params=pltpu.CompilerParams(vmem_limit_bytes=VMEM_LIMIT),
        cost_estimate=cost(4, rows, depth, span[1] - span[0]),
        name="post",
    )(*operands)
    return out[:3], (out[3], out[4]), out[5]


def finish_kernel(own, first, second, zero, out):
    gate, up, d_hidden = (
        own[:, n] + first[:, n].astype(F32) + (second[:, n].astype(F32) + zero[1]) for n in range(3)
    )
    sigmoid = 1.0 / (1.0 + jnp.exp(-gate))
    active = gate * sigmoid
    out[:, 0] = (active * up).astype(BF16)
    out[:, 1] = (d_hidden * up * sigmoid * (1.0 + gate * (1.0 - sigmoid))).astype(BF16)
    out[:, 2] = (d_hidden * active).astype(BF16)


def finished(*operands):
    shape = operands[0].shape
    return pl.pallas_call(
        finish_kernel,
        in_specs=[VMEM] * 4,
        out_specs=VMEM,
        out_shape=pltpu.VMEM(shape, BF16),
        compiler_params=pltpu.CompilerParams(vmem_limit_bytes=VMEM_LIMIT),
        cost_estimate=pl.CostEstimate(flops=0, bytes_accessed=1000, transcendentals=0),
        name="finish",
    )(*[near_core(v) for v in operands])


def activations(gate, up, d_hidden):
    sigmoid = jax.nn.sigmoid(gate)
    active = gate * sigmoid
    hidden = (active * up).astype(BF16)
    d_gate = (d_hidden * up * sigmoid * (1.0 + gate * (1.0 - sigmoid))).astype(BF16)
    d_up = (d_hidden * active).astype(BF16)
    return jnp.stack([hidden, d_gate, d_up], 1)


def chunk_plan(units):
    starts = list(range(0, units, SUB))
    one, two = [[(0, s)] for s in starts], [[(1, s)] for s in starts]
    return one[:1] + two + one[1:]


def block_table(plan, steps, experts):
    rows, spans = [], {}
    for name, k in steps:
        if name not in ("partial", "post"):
            continue
        base = len(rows)
        for unit, (group, start) in enumerate(plan[k]):
            ranks = [0] if group == 0 else list(range(1, experts))
            for rank in ranks:
                rows.append((rank, unit, group, start, int(rank == ranks[0]), int(rank == ranks[-1])))
        spans[name, k] = (base, len(rows))
    return rows, spans


def sequence(count):
    if count != 8:
        return [(name, k) for k in range(count) for name in ("partial", "merge", "finish", "post")]
    return [(STEPS[word[0]], int(word[1:])) for word in ORDER]


STEPS = {"P": "partial", "M": "merge", "F": "finish", "Q": "post"}
ORDER = (
    "P0", "P1", "P2", "M0", "P3", "M1", "F0", "P4", "M2", "F1", "P5", "Q0",
    "M3", "F2", "Q1", "M4", "F3", "P6", "M5", "P7", "F4", "Q2", "F5", "M6",
    "Q3", "M7", "F6", "Q4", "F7", "Q5", "Q6", "Q7",
)


def on_device(sections, parts, tokens, combine, expert_ids, expert_counts, w_gate, w_up, w_down, cotangent):
    total = combine.shape[0]
    local = tokens.shape[0]
    experts = w_gate.shape[0]
    weights = (w_gate, w_up, w_down)
    chips = parts // 2
    me = lax.axis_index("tensor")
    place = lax.axis_index("section")
    chip, core = me // 2, me % 2

    pair = jnp.stack([tokens, cotangent], 0)
    near = jnp.concatenate(
        [pair]
        + [lax.ppermute(pair, "tensor", [(i, (i - 2 * n) % parts) for i in range(parts)]) for n in range(1, chips)],
        1,
    )
    swap = [(i, i ^ 1) for i in range(parts)]
    far = lax.ppermute(near, "tensor", swap)
    full = jnp.concatenate([near, far], 1)
    x, cot = full[0], full[1]

    def turned(v):
        v = v.reshape(chips, 2, local, v.shape[1])
        v = jnp.where(core == 1, v[:, ::-1], v).transpose(1, 0, 2, 3)
        v = lax.dynamic_slice_in_dim(jnp.concatenate([v, v], 1), chip, chips, 1)
        return v.reshape(total, v.shape[3])

    scale, ids = turned(combine), turned(expert_ids)
    common = jnp.argmax(expert_counts).astype(jnp.int32)
    is_first = ids[:, :1] == common
    other = jnp.where(is_first, ids[:, 1:], ids[:, :1])
    weight = jnp.stack(
        [
            jnp.where(is_first, scale[:, :1], scale[:, 1:]),
            jnp.where(is_first, scale[:, 1:], scale[:, :1]),
        ],
        0,
    )
    rg = (weight * cot.astype(F32)[None]).astype(BF16)

    plan = chunk_plan(w_gate.shape[2])
    count = len(plan)
    steps = sequence(count)
    blocks, spans = block_table(plan, steps, experts)
    line = sections == 4
    edge = jnp.logical_or(place == 0, place == sections - 1) if line else jnp.zeros((), bool)
    lane = jnp.arange(128, dtype=jnp.int32)
    head = jnp.where(lane == 0, common, lane - (lane <= common).astype(jnp.int32))
    head = jnp.where(lane == 127, edge.astype(jnp.int32), head)[None]

    own, sent, first, mine, came = {}, {}, {}, {}, {}
    state = None
    slots = preload(blocks, head, weights)
    after = ()

    def send(v, pairs):
        return lax.ppermute(v, "section", pairs)

    for name, k in steps:
        if name == "partial":
            slots, own[k], packed, zero = partial_products(
                spans[name, k], len(plan[k]), blocks, head, x, rg, other, weights, slots, after
            )
            sent[k] = send(packed, [(0, 1), (3, 2)]) if line else None
            after = (zero,)
        elif name == "merge" and line:
            first[k] = sent[k]
            packed = (own[k] + (sent[k].astype(F32) + zero[0])).astype(BF16)
            sent[k] = send(packed, [(1, 2), (2, 1)])
            after += (packed,)
        elif name == "finish" and line:
            mine[k] = finished(own[k], first[k], sent[k], zero)
            came[k] = send(mine[k], [(1, 0), (2, 3)])
            after += (mine[k],)
        elif name == "finish":
            all_of = lax.psum(own[k], "section")
            mine[k] = came[k] = activations(all_of[:, 0], all_of[:, 1], all_of[:, 2])
        elif name == "post":
            slots, state, zero = post_products(
                spans[name, k], blocks, head, mine[k], came[k], rg, weight, other, weights, slots, state,
                after, k == count - 1,
            )
            after = (zero,)
    (d_down, give), keep = state, zero
    both = keep + lax.ppermute(give, "tensor", swap).astype(F32)
    result = both[:, :local]
    for n in range(1, chips):
        piece = both[:, n * local : (n + 1) * local].astype(BF16)
        result += lax.ppermute(piece, "tensor", [(i, (i + 2 * n) % parts) for i in range(parts)]).astype(F32)
    return result[0].astype(BF16), result[1].astype(BF16), d_down


def solution(mesh):
    in_specs = (
        P("tensor", "section"),
        P(),
        P(),
        P(),
        P(None, "section", "tensor"),
        P(None, "section", "tensor"),
        P(None, "tensor", "section"),
        P("tensor", "section"),
    )
    out_specs = (P("tensor", "section"), P("tensor", "section"), P(None, "tensor", "section"))
    return jax.shard_map(
        functools.partial(on_device, mesh.shape["section"], mesh.shape["tensor"]),
        mesh=mesh,
        in_specs=in_specs,
        out_specs=out_specs,
        check_vma=False,
    )
```

```python
import functools

import jax
import jax.numpy as jnp
from jax import lax
from jax.experimental import pallas as pl
from jax.experimental.pallas import tpu as pltpu
from jax.sharding import PartitionSpec as P

SUB = 512
EARLY = 2
SLOTS = EARLY + 1
F32 = jnp.float32
BF16 = jnp.bfloat16
COST_FACTOR = 4.0
VMEM_LIMIT = 20 * 1024 * 1024
ANY = pl.BlockSpec(memory_space=pl.ANY)
HBM = pl.BlockSpec(memory_space=pltpu.HBM)
VMEM = pl.BlockSpec(memory_space=pltpu.VMEM)
EXPERT, UNIT, GROUP, COLUMN, FIRST, LAST, FIELDS = 0, 1, 2, 3, 4, 5, 6


def dot(a, b, contract):
    return lax.dot_general(a, b, ((contract[0], contract[1]), ((), ())), preferred_element_type=F32)


def fill_table(rows, base, head, table):
    order = {rank: head[0, rank] for rank in sorted({row[EXPERT] for row in rows})}
    for n, row in enumerate(rows):
        for field, value in enumerate(row):
            table[n * FIELDS + field] = order[value] if field == EXPERT else value
    return lambda i, field: table[(i - base) * FIELDS + field]


def weight_copies(field, i, weights, buffers, sems):
    slot = lax.rem(i, SLOTS)
    expert = field(i, EXPERT)
    units = pl.ds(pl.multiple_of(field(i, COLUMN), SUB), SUB)
    wg, wu, wd = weights
    return (
        pltpu.make_async_copy(wg.at[expert, :, units], buffers[0].at[slot], sems.at[slot, 0]),
        pltpu.make_async_copy(wu.at[expert, :, units], buffers[1].at[slot], sems.at[slot, 1]),
        pltpu.make_async_copy(wd.at[expert, units, :], buffers[2].at[slot], sems.at[slot, 2]),
    )


def begin_all(copies):
    for copy in copies:
        copy.start()


def wait_all(copies):
    for copy in copies:
        copy.wait()


def preload_kernel(rows, head, wg, wu, wd, b0, b1, b2, table, wsem):
    field = fill_table(rows, 0, head, table)
    copies = [weight_copies(field, i, (wg, wu, wd), (b0, b1, b2), wsem) for i in range(len(rows))]
    for copy in copies:
        begin_all(copy)
    for copy in copies:
        wait_all(copy)


def over_blocks(span, total, fetch, work):
    base, end, ready, ahead = span
    stop = min(end + ahead, total)
    for i in range(base + ready, min(base + EARLY, stop)):
        begin_all(fetch(i))

    def body(i, carry):
        @pl.when(i + EARLY < stop)
        def _():
            begin_all(fetch(i + EARLY))

        @pl.when(i >= base + ready)
        def _():
            wait_all(fetch(i))

        work(i)
        return carry

    lax.fori_loop(base, end, body, 0)
    for i in range(max(end, base + ready), stop):
        wait_all(fetch(i))


def partial_kernel(span, total, rows, deps, head, other, x, rg, wg, wu, wd, *rest):
    b0, b1, b2, own, send, zero, table, wsem = rest[deps + 3 :]
    field = fill_table(rows, span[0], head, table)
    fetch = lambda i: weight_copies(field, i, (wg, wu, wd), (b0, b1, b2), wsem)
    zero[...] = jnp.zeros_like(zero)

    def work(i):
        slot, unit, group = lax.rem(i, SLOTS), field(i, UNIT), field(i, GROUP)
        keep = jnp.logical_or(other[...] == field(i, EXPERT), field(i, FIRST) == 1)
        terms = (
            dot(x[...], b0[slot], ((1,), (0,))),
            dot(x[...], b1[slot], ((1,), (0,))),
            dot(rg[group], b2[slot], ((1,), (1,))),
        )
        for n, term in enumerate(terms):
            own[unit, n] = jnp.where(keep, term, own[unit, n])

        @pl.when(field(i, LAST) == 1)
        def _():
            for n in range(3):
                send[unit, n] = own[unit, n].astype(BF16)

    over_blocks(span, total, fetch, work)


def near_core(v):
    return pltpu.with_memory_space_constraint(v, pltpu.VMEM)


def slot_shapes(depth):
    return [pltpu.VMEM((SLOTS, depth, SUB), BF16)] * 2 + [pltpu.VMEM((SLOTS, SUB, depth), BF16)]


def in_hbm(v):
    return pltpu.with_memory_space_constraint(v, pltpu.HBM)


def cost(products, rows, depth, blocks):
    return pl.CostEstimate(
        flops=int(2 * products * rows * depth * SUB * blocks * COST_FACTOR),
        bytes_accessed=int(6 * depth * SUB * blocks * COST_FACTOR),
        transcendentals=0,
    )


def preload(blocks, head, weights):
    depth = weights[0].shape[1]
    return pl.pallas_call(
        functools.partial(preload_kernel, blocks[:EARLY]),
        in_specs=[VMEM] + [HBM] * 3,
        out_specs=[VMEM] * 3,
        out_shape=slot_shapes(depth),
        scratch_shapes=[pltpu.SMEM((EARLY * FIELDS,), jnp.int32), pltpu.SemaphoreType.DMA((SLOTS, 3))],
        compiler_params=pltpu.CompilerParams(vmem_limit_bytes=VMEM_LIMIT),
        cost_estimate=cost(0, 0, depth, EARLY),
        name="preload",
    )(near_core(head), *[in_hbm(w) for w in weights])


def partial_products(span, units, blocks, head, x, rg, other, weights, slots, after):
    depth = weights[0].shape[1]
    rows = x.shape[0]
    shape = (units, 3, rows, SUB)
    seen = blocks[span[0] : span[1] + EARLY]
    operands = [near_core(v) for v in (head, other, x, rg)] + [in_hbm(w) for w in weights] + list(after)
    in_specs = [VMEM] * 4 + [HBM] * 3 + [ANY] * len(after) + [VMEM] * 3
    aliases = {len(operands) + n: n for n in range(3)}
    operands += [near_core(v) for v in slots]
    out = pl.pallas_call(
        functools.partial(partial_kernel, span, len(blocks), seen, len(after)),
        in_specs=in_specs,
        out_specs=[VMEM] * 6,
        scratch_shapes=[pltpu.SMEM((len(seen) * FIELDS,), jnp.int32), pltpu.SemaphoreType.DMA((SLOTS, 3))],
        out_shape=slot_shapes(depth) + [pltpu.VMEM(shape, F32), pltpu.VMEM(shape, BF16), pltpu.VMEM((2, 1, SUB), F32)],
        input_output_aliases=aliases,
        compiler_params=pltpu.CompilerParams(vmem_limit_bytes=VMEM_LIMIT),
        cost_estimate=cost(3, rows, depth, span[1] - span[0]),
        name="partial",
    )(*operands)
    return out[:3], out[3], out[4], out[5]


def post_kernel(span, total, rows, deps, opening, closing, head, other, weight, mine, came, rg, wg, wu, wd, *rest):
    rest = rest[deps + 3 :]
    if not opening:
        sums_in, rest = rest[0], rest[2:]
    b0, b1, b2, d_down, sums, extra = rest[:6]
    ddv, table, wsem, dsem = rest[-4:]
    base, end = span[:2]
    field = fill_table(rows, base, head, table)
    edge = head[0, head.shape[1] - 1]
    fetch = lambda i: weight_copies(field, i, (wg, wu, wd), (b0, b1, b2), wsem)
    if closing:
        give, sums = sums, rest[6]
        sums[...] = jnp.zeros_like(sums) if opening else sums_in[...]
    else:
        extra[...] = jnp.zeros_like(extra)
        if opening:
            sums[...] = jnp.zeros_like(sums)

    def leave(i):
        slot = lax.rem(i, 2)
        units = pl.ds(pl.multiple_of(field(i, COLUMN), SUB), SUB)
        return pltpu.make_async_copy(ddv.at[slot], d_down.at[field(i, EXPERT), units, :], dsem.at[slot])

    def work(i):
        @pl.when(i >= base + 2)
        def _():
            leave(i - 2).wait()

        slot, unit, group = lax.rem(i, SLOTS), field(i, UNIT), field(i, GROUP)
        keep = jnp.logical_or(other[...] == field(i, EXPERT), group == 0)
        use_came = jnp.logical_and(keep, edge == 1)
        use_mine = jnp.logical_and(keep, edge == 0)
        hidden, d_gate, d_up = (
            jnp.where(use_came, came[unit, n], jnp.where(use_mine, mine[unit, n], jnp.zeros(mine.shape[2:], BF16)))
            for n in range(3)
        )
        ddv[lax.rem(i, 2)] = dot(hidden, rg[group], ((0,), (0,))).astype(BF16)
        leave(i).start()
        sums[0] += weight[group] * dot(hidden, b2[slot], ((1,), (0,)))
        sums[1] += dot(d_gate, b0[slot], ((1,), (1,))) + dot(d_up, b1[slot], ((1,), (1,)))

    over_blocks(span, total, fetch, work)
    if closing:
        half = sums.shape[1] // 2
        give[...] = sums[:, half:].astype(BF16)
        extra[...] = sums[:, :half]
    for i in range(max(end - 2, base), end):
        leave(i).wait()


def post_products(span, blocks, head, mine, came, rg, weight, other, weights, slots, state, after, closing):
    experts, depth, width = weights[0].shape
    rows = rg.shape[1]
    opening = state is None
    seen = blocks[span[0] : span[1] + EARLY]
    operands = [near_core(v) for v in (head, other, weight, mine, came, rg)] + [in_hbm(w) for w in weights]
    operands += list(after)
    in_specs = [VMEM] * 6 + [HBM] * 3 + [ANY] * len(after) + [VMEM] * 3
    aliases = {len(operands) + n: n for n in range(3)}
    operands += [near_core(v) for v in slots]
    if not opening:
        aliases[len(operands) + 1] = 3
        if not closing:
            aliases[len(operands)] = 4
        in_specs += [VMEM, HBM]
        operands += [near_core(state[1]), in_hbm(state[0])]
    sums_shape = pltpu.VMEM((2, rows, depth), F32)
    out_shape = slot_shapes(depth) + [pltpu.HBM((experts, width, depth), BF16)]
    if closing:
        out_shape += [pltpu.VMEM((2, rows // 2, depth), kind) for kind in (BF16, F32)]
    else:
        out_shape += [sums_shape, pltpu.VMEM((2, 1, SUB), F32)]
    out = pl.pallas_call(
        functools.partial(post_kernel, span, len(blocks), seen, len(after), opening, closing),
        in_specs=in_specs,
        out_specs=[VMEM] * 3 + [HBM, VMEM, VMEM],
        scratch_shapes=([sums_shape] if closing else [])
        + [
            pltpu.VMEM((2, SUB, depth), BF16),
            pltpu.SMEM((len(seen) * FIELDS,), jnp.int32),
            pltpu.SemaphoreType.DMA((SLOTS, 3)),
            pltpu.SemaphoreType.DMA((2,)),
        ],
        out_shape=out_shape,
        input_output_aliases=aliases,
        compiler_params=pltpu.CompilerParams(vmem_limit_bytes=VMEM_LIMIT),
        cost_estimate=cost(4, rows, depth, span[1] - span[0]),
        name="post",
    )(*operands)
    return out[:3], (out[3], out[4]), out[5]


def finish_kernel(own, first, second, zero, out):
    gate, up, d_hidden = (
        own[:, n] + first[:, n].astype(F32) + (second[:, n].astype(F32) + zero[1]) for n in range(3)
    )
    sigmoid = 1.0 / (1.0 + jnp.exp(-gate))
    active = gate * sigmoid
    out[:, 0] = (active * up).astype(BF16)
    out[:, 1] = (d_hidden * up * sigmoid * (1.0 + gate * (1.0 - sigmoid))).astype(BF16)
    out[:, 2] = (d_hidden * active).astype(BF16)


def finished(*operands):
    shape = operands[0].shape
    return pl.pallas_call(
        finish_kernel,
        in_specs=[VMEM] * 4,
        out_specs=VMEM,
        out_shape=pltpu.VMEM(shape, BF16),
        compiler_params=pltpu.CompilerParams(vmem_limit_bytes=VMEM_LIMIT),
        cost_estimate=pl.CostEstimate(flops=0, bytes_accessed=1000, transcendentals=0),
        name="finish",
    )(*[near_core(v) for v in operands])


def activations(gate, up, d_hidden):
    sigmoid = jax.nn.sigmoid(gate)
    active = gate * sigmoid
    hidden = (active * up).astype(BF16)
    d_gate = (d_hidden * up * sigmoid * (1.0 + gate * (1.0 - sigmoid))).astype(BF16)
    d_up = (d_hidden * active).astype(BF16)
    return jnp.stack([hidden, d_gate, d_up], 1)


def chunk_plan(units):
    starts = list(range(0, units, SUB))
    one, two = [[(0, s)] for s in starts], [[(1, s)] for s in starts]
    return one[:1] + two + one[1:]


def block_table(plan, steps, experts):
    rows, spans, ready = [], {}, EARLY
    for name, k in steps:
        if name not in ("partial", "post"):
            continue
        base = len(rows)
        for unit, (group, start) in enumerate(plan[k]):
            ranks = [0] if group == 0 else list(range(1, experts))
            for rank in ranks:
                rows.append((rank, unit, group, start, int(rank == ranks[0]), int(rank == ranks[-1])))
        ahead = EARLY if name == "post" and len(rows) - base > 1 else 1
        spans[name, k] = (base, len(rows), ready, ahead)
        ready = ahead
    return rows, spans


def sequence(count):
    if count != 8:
        return [(name, k) for k in range(count) for name in ("partial", "merge", "finish", "post")]
    return [(STEPS[word[0]], int(word[1:])) for word in ORDER]


STEPS = {"P": "partial", "M": "merge", "F": "finish", "Q": "post"}
ORDER = (
    "P0", "P1", "P2", "M0", "P3", "M1", "F0", "P4", "M2", "F1", "P5", "Q0",
    "M3", "F2", "Q1", "M4", "F3", "P6", "M5", "P7", "F4", "Q2", "F5", "M6",
    "Q3", "M7", "F6", "Q4", "F7", "Q5", "Q6", "Q7",
)


def on_device(sections, parts, tokens, combine, expert_ids, expert_counts, w_gate, w_up, w_down, cotangent):
    total = combine.shape[0]
    local = tokens.shape[0]
    experts = w_gate.shape[0]
    weights = (w_gate, w_up, w_down)
    chips = parts // 2
    me = lax.axis_index("tensor")
    place = lax.axis_index("section")
    chip, core = me // 2, me % 2

    pair = jnp.stack([tokens, cotangent], 0)
    near = jnp.concatenate(
        [pair]
        + [lax.ppermute(pair, "tensor", [(i, (i - 2 * n) % parts) for i in range(parts)]) for n in range(1, chips)],
        1,
    )
    swap = [(i, i ^ 1) for i in range(parts)]
    far = lax.ppermute(near, "tensor", swap)
    full = jnp.concatenate([near, far], 1)
    x, cot = full[0], full[1]

    def turned(v):
        v = v.reshape(chips, 2, local, v.shape[1])
        v = jnp.where(core == 1, v[:, ::-1], v).transpose(1, 0, 2, 3)
        v = lax.dynamic_slice_in_dim(jnp.concatenate([v, v], 1), chip, chips, 1)
        return v.reshape(total, v.shape[3])

    scale, ids = turned(combine), turned(expert_ids)
    common = jnp.argmax(expert_counts).astype(jnp.int32)
    is_first = ids[:, :1] == common
    other = jnp.where(is_first, ids[:, 1:], ids[:, :1])
    weight = jnp.stack(
        [
            jnp.where(is_first, scale[:, :1], scale[:, 1:]),
            jnp.where(is_first, scale[:, 1:], scale[:, :1]),
        ],
        0,
    )
    rg = (weight * cot.astype(F32)[None]).astype(BF16)

    plan = chunk_plan(w_gate.shape[2])
    count = len(plan)
    steps = sequence(count)
    blocks, spans = block_table(plan, steps, experts)
    line = sections == 4
    edge = jnp.logical_or(place == 0, place == sections - 1) if line else jnp.zeros((), bool)
    lane = jnp.arange(128, dtype=jnp.int32)
    head = jnp.where(lane == 0, common, lane - (lane <= common).astype(jnp.int32))
    head = jnp.where(lane == 127, edge.astype(jnp.int32), head)[None]

    own, sent, first, mine, came = {}, {}, {}, {}, {}
    state = None
    slots = preload(blocks, head, weights)
    after = ()

    def send(v, pairs):
        return lax.ppermute(v, "section", pairs)

    for name, k in steps:
        if name == "partial":
            slots, own[k], packed, zero = partial_products(
                spans[name, k], len(plan[k]), blocks, head, x, rg, other, weights, slots, after
            )
            sent[k] = send(packed, [(0, 1), (3, 2)]) if line else None
            after = (zero,)
        elif name == "merge" and line:
            first[k] = sent[k]
            packed = (own[k] + (sent[k].astype(F32) + zero[0])).astype(BF16)
            sent[k] = send(packed, [(1, 2), (2, 1)])
            after += (packed,)
        elif name == "finish" and line:
            mine[k] = finished(own[k], first[k], sent[k], zero)
            came[k] = send(mine[k], [(1, 0), (2, 3)])
            after += (mine[k],)
        elif name == "finish":
            all_of = lax.psum(own[k], "section")
            mine[k] = came[k] = activations(all_of[:, 0], all_of[:, 1], all_of[:, 2])
        elif name == "post":
            slots, state, zero = post_products(
                spans[name, k], blocks, head, mine[k], came[k], rg, weight, other, weights, slots, state,
                after, k == count - 1,
            )
            after = (zero,)
    (d_down, give), keep = state, zero
    both = keep + lax.ppermute(give, "tensor", swap).astype(F32)
    result = both[:, :local]
    for n in range(1, chips):
        piece = both[:, n * local : (n + 1) * local].astype(BF16)
        result += lax.ppermute(piece, "tensor", [(i, (i + 2 * n) % parts) for i in range(parts)]).astype(F32)
    return result[0].astype(BF16), result[1].astype(BF16), d_down


def solution(mesh):
    in_specs = (
        P("tensor", "section"),
        P(),
        P(),
        P(),
        P(None, "section", "tensor"),
        P(None, "section", "tensor"),
        P(None, "tensor", "section"),
        P("tensor", "section"),
    )
    out_specs = (P("tensor", "section"), P("tensor", "section"), P(None, "tensor", "section"))
    return jax.shard_map(
        functools.partial(on_device, mesh.shape["section"], mesh.shape["tensor"]),
        mesh=mesh,
        in_specs=in_specs,
        out_specs=out_specs,
        check_vma=False,
    )
```
